768 devices in a mesh: dp: 192 (over z, y_lo, x), rows: 4 (over y_hi, core).
Axes of the slice: x: 4, y: 8 (y_hi: 2, y_lo: 4; y = y_hi * 4 + y_lo), z: 12, core: 2. Of those that a mesh axis runs over, the one named last changes fastest.
Arguments:
- images: bfloat16 [98304, 1152], P(('dp', 'rows')), may hold values from -5 to 5
- texts: bfloat16 [98304, 1152], P(('dp', 'rows')), may hold values from -5 to 5
- positive_offset: int32 [98304], P(('dp', 'rows')), may hold values from 0 to 5
- logit_log_scale: float32 [1], replicated, may hold values from 1.6 to 2.6
- bias: float32 [1], replicated, may hold values from -4 to -2
Outputs:
- image_gradient: float32 [98304, 1152], P(('dp', 'rows'))
- text_gradient: float32 [98304, 1152], P(('dp', 'rows'))
The draws below stay inside these ranges and needn't reach their ends.
All inputs are finite; a program needn't handle non-finite values.
Results may differ from the reference program's by a relative error of at most 0.004.
Values may be sent and summed in bfloat16 or wider, within the bound.
No kernel may reach another device: no remote copies, remote signals or barrier semaphores. Data moves between devices by JAX's collectives and lax.ppermute only.
A program may use at most 32 MiB of HBM per device.

```python
import math
import jax
import jax.numpy as jnp
from jax import lax

EMBED_WIDTH = 1152
STEPS = 6
GROUP = 512
GROUPS = 192
TOTAL_PAIRS = 98304


def shape_rows(noise, key, row_low, row_high):
    row_key, column_key = jax.random.split(key, 2)
    row_scale = jnp.exp(jax.random.uniform(row_key, (TOTAL_PAIRS, 1), jnp.float32, math.log(row_low), math.log(row_high)))
    column_scale = jnp.exp(jax.random.uniform(column_key, (1, EMBED_WIDTH), jnp.float32, math.log(0.5), math.log(2.0)))
    return noise * column_scale * row_scale / math.sqrt(EMBED_WIDTH)


def draw_images(key, part):
    key = jax.random.fold_in(key, 11)
    noise_key, shape_key = jax.random.split(key)
    noise = jnp.clip(jax.random.normal(noise_key, (TOTAL_PAIRS, EMBED_WIDTH), jnp.float32), -6.0, 6.0)
    values = shape_rows(noise, shape_key, 0.3, 3.0)
    return values.astype(jnp.bfloat16)


def draw_texts(key, part):
    key = jax.random.fold_in(key, 12)
    noise_key, shape_key = jax.random.split(key)
    noise = jnp.clip(jax.random.normal(noise_key, (TOTAL_PAIRS, EMBED_WIDTH), jnp.float32), -6.0, 6.0)
    values = shape_rows(noise, shape_key, 0.3, 3.0)
    return values.astype(jnp.bfloat16)


def plant(drawn, rng, low, high):
    dims = drawn.shape
    place = [jax.random.randint(jax.random.fold_in(rng, axis), (), 0, dims[axis]) for axis in range(len(dims))]
    drawn = drawn.at[tuple(place)].set(low)
    longest = dims.index(max(dims))
    place[longest] = (place[longest] + 1) % dims[longest]
    return drawn.at[tuple(place)].set(high)


def setup_inputs(seed: int = 0) -> dict:
    key_list = jax.random.split(jax.random.key(seed), 6)
    images = draw_images(jax.random.fold_in(key_list[5], 71), 0)
    texts = draw_texts(jax.random.fold_in(key_list[5], 71), 0)
    positive_offset = plant(jax.random.randint(key_list[2], (TOTAL_PAIRS,), 0, STEPS), jax.random.fold_in(key_list[2], 1), 0, STEPS - 1).astype(jnp.int32)
    logit_log_scale = jnp.clip(jax.random.uniform(key_list[3], (1,), jnp.float32, 1.6, 2.6), 1.6, 2.6)
    bias = jnp.clip(jax.random.uniform(key_list[4], (1,), jnp.float32, -4.0, -2.0), -4.0, -2.0)
    return dict(images=images, texts=texts, positive_offset=positive_offset, logit_log_scale=logit_log_scale, bias=bias)


def unit_rows(values):
    widened = values.astype(jnp.float32)
    row_norm = jnp.sqrt(lax.optimization_barrier(jnp.sum(widened * widened, axis=1, keepdims=True)) + 1e-06)
    return (widened / row_norm, row_norm)

def project_tangent(unit_values, row_norm, direction):
    inner = lax.optimization_barrier(jnp.sum(unit_values * direction, axis=1, keepdims=True))
    return (direction - unit_values * inner) / row_norm

def reference(images, texts, positive_offset, logit_log_scale, bias):
    unit_image_rows, image_norm_values = unit_rows(images)
    unit_text_rows, text_norm_values = unit_rows(texts)
    image_low = lax.optimization_barrier(unit_image_rows.astype(jnp.bfloat16)).astype(jnp.float32)
    text_low = lax.optimization_barrier(unit_text_rows.astype(jnp.bfloat16)).astype(jnp.float32)
    image_block_list = image_low.reshape(GROUPS, GROUP, EMBED_WIDTH)
    text_blocks = text_low.reshape(GROUPS, GROUP, EMBED_WIDTH)
    logit_scale_value = jnp.exp(logit_log_scale[0])
    logit_bias = bias[0]
    half_window = STEPS // 2
    target = (positive_offset - (half_window - 1)).reshape(GROUPS, GROUP)
    diagonal = jnp.arange(GROUP)[:, None] == jnp.arange(GROUP)[None, :]
    image_total_sum = jnp.zeros((GROUPS, GROUP, EMBED_WIDTH), jnp.float32)
    text_total_sum = jnp.zeros((GROUPS, GROUP, EMBED_WIDTH), jnp.float32)
    for offset in range(1 - half_window, half_window + 1):
        paired_side = jnp.roll(text_blocks, -offset, axis=0)
        pair_logits = logit_scale_value * jnp.einsum('lba,lma->lbm', image_block_list, paired_side, precision=lax.Precision.HIGHEST) + logit_bias
        positive = jnp.logical_and(target[:, :, None] == offset, diagonal[None, :, :])
        label_sign = jnp.where(positive, 1.0, -1.0).astype(jnp.float32)
        pair_weights = lax.optimization_barrier((-label_sign * jax.nn.sigmoid(-label_sign * pair_logits)).astype(jnp.bfloat16)).astype(jnp.float32)
        image_total_sum = image_total_sum + jnp.einsum('mtp,mpd->mtd', pair_weights, paired_side, precision=lax.Precision.HIGHEST)
        text_portion = jnp.einsum('ghf,ghq->gfq', pair_weights, image_block_list, precision=lax.Precision.HIGHEST)
        text_total_sum = text_total_sum + jnp.roll(text_portion, offset, axis=0)
    image_gradient = project_tangent(unit_image_rows, image_norm_values, logit_scale_value * image_total_sum.reshape(TOTAL_PAIRS, EMBED_WIDTH))
    text_gradient = project_tangent(unit_text_rows, text_norm_values, logit_scale_value * text_total_sum.reshape(TOTAL_PAIRS, EMBED_WIDTH))
    return (image_gradient, text_gradient)
```

```python
import jax
import jax.numpy as jnp
from jax import lax
from jax.sharding import PartitionSpec as P


def from_group(block, distance):
    count = lax.axis_size("dp")
    return lax.ppermute(block, "dp", [((i + distance) % count, i) for i in range(count)])


def from_member(block, flip):
    return lax.ppermute(block, "rows", [(i ^ flip, i) for i in range(lax.axis_size("rows"))])


def unit_rows(values):
    widened = values.astype(jnp.float32)
    row_norm = jnp.sqrt(jnp.sum(widened * widened, axis=1, keepdims=True) + 1e-06)
    return widened / row_norm, row_norm


def low_rows(values):
    return unit_rows(values)[0].astype(jnp.bfloat16)


def project_tangent(unit_values, row_norm, direction):
    inner = jnp.sum(unit_values * direction, axis=1, keepdims=True)
    return (direction - unit_values * inner) / row_norm


def local(images, texts, positive_offset, logit_log_scale, bias):
    low = jnp.bfloat16
    quarter = texts.shape[0]
    scale = jnp.exp(logit_log_scale[0])
    target = positive_offset - 2

    images_far = from_member(images, 2)
    texts_at = {0: texts}
    texts_at[1] = from_group(texts, 1)
    texts_at[-1] = from_group(texts, -1)
    texts_at[3] = from_group(texts, 3)
    images_near = from_member(images, 1)
    images_far_near = from_member(images_far, 1)
    texts_at[2] = from_group(texts_at[1], 1)
    texts_at[-2] = from_group(texts_at[-1], -1)

    group = low_rows(jnp.concatenate([images, images_near, images_far, images_far_near]))
    diagonal = jnp.arange(group.shape[0])[:, None] == jnp.arange(quarter)[None, :]

    image_sum = jnp.zeros(group.shape, jnp.float32)
    text_part = {}
    for offset in (0, 1, -1, 3, 2, -2):
        text = low_rows(texts_at[offset])
        scores = lax.dot_general(
            group, text, (((1,), (1,)), ((), ())), preferred_element_type=jnp.float32
        )
        logits = scale * scores + bias[0]
        positive = jnp.logical_and((target == offset)[None, :], diagonal)
        sign = jnp.where(positive, 1.0, -1.0).astype(jnp.float32)
        weights = (-sign * jax.nn.sigmoid(-sign * logits)).astype(low)
        image_sum = image_sum + jnp.dot(weights, text, preferred_element_type=jnp.float32)
        text_part[offset] = lax.dot_general(
            weights, group, (((0,), (0,)), ((), ())), preferred_element_type=jnp.float32
        )

    def home(part, distance):
        return from_group(part.astype(low), -distance).astype(jnp.float32)

    above = text_part[1] + home(text_part[2], 1)
    below = text_part[-1] + home(text_part[-2], -1)
    text_total = text_part[0] + home(text_part[3], 3) + home(above, 1) + home(below, -1)

    parts = image_sum.reshape(4, quarter, -1)
    near = from_member(parts[1::2].astype(low), 1).astype(jnp.float32)
    parts = parts[0::2] + near
    image_total = parts[0] + from_member(parts[1].astype(low), 2).astype(jnp.float32)

    image_gradient = project_tangent(*unit_rows(images), scale * image_total)
    text_gradient = project_tangent(*unit_rows(texts), scale * text_total)
    return image_gradient, text_gradient


def solution(mesh):
    return jax.shard_map(
        local,
        mesh=mesh,
        in_specs=(P(("dp", "rows"), None), P(("dp", "rows"), None), P(("dp", "rows")), P(), P()),
        out_specs=(P(("dp", "rows"), None), P(("dp", "rows"), None)),
        check_vma=False,
    )
```

```python
import jax
import jax.numpy as jnp
from jax import lax
from jax.experimental import pallas as pl
from jax.experimental.pallas import tpu as pltpu
from jax.sharding import PartitionSpec as P

MEMBERS = 4
VMEM = pl.BlockSpec(memory_space=pltpu.VMEM)
SMEM = pl.BlockSpec(memory_space=pltpu.SMEM)
LIMIT = 32 << 20
LOW, WIDE = jnp.bfloat16, jnp.float32


def from_member(block, flip):
    return lax.ppermute(block, "rows", [(i ^ flip, i) for i in range(MEMBERS)])


def from_group(block, distance):
    count = lax.axis_size("dp")
    return lax.ppermute(block, "dp", [((i + distance) % count, i) for i in range(count)])


def kernel_call(body, outs, *args):
    return pl.pallas_call(
        body,
        out_shape=[jax.ShapeDtypeStruct(s, d) for s, d in outs],
        in_specs=[SMEM if a.ndim == 1 else VMEM for a in args],
        out_specs=[VMEM] * len(outs),
        compiler_params=pltpu.CompilerParams(vmem_limit_bytes=LIMIT),
        cost_estimate=pl.CostEstimate(flops=0, bytes_accessed=0, transcendentals=0),
    )(*args)


def unit_rows(raw):
    wide = raw.astype(WIDE)
    inverse = lax.rsqrt(jnp.sum(wide * wide, axis=1, keepdims=True) + 1e-06)
    return wide * inverse, inverse


def tangent(unit, direction):
    return direction - unit * jnp.sum(unit * direction, axis=1, keepdims=True)


def sigmoid(values):
    return 1.0 / (1.0 + jnp.exp(-values))


def meet(group, text, scalars, target, offsets):
    quarter = target.shape[1]
    scores = lax.dot_general(
        group, text, (((1,), (1,)), ((), ())), preferred_element_type=WIDE
    )
    logits = scalars[0] * scores + scalars[1]
    row = lax.broadcasted_iota(jnp.int32, (quarter, quarter), 0)
    diagonal = row == lax.broadcasted_iota(jnp.int32, (quarter, quarter), 1)
    own = []
    for i, offset in enumerate(offsets):
        block = logits[:quarter, i * quarter : (i + 1) * quarter]
        sign = jnp.where(jnp.logical_and(diagonal, target == offset), -1.0, 1.0)
        own.append(sign * sigmoid(sign * block))
    own = jnp.concatenate(own, axis=1).astype(LOW)
    weights = jnp.concatenate([own, sigmoid(logits[quarter:]).astype(LOW)])
    image_part = jnp.dot(weights, text, preferred_element_type=WIDE)
    text_part = lax.dot_general(
        weights, group, (((0,), (0,)), ((), ())), preferred_element_type=WIDE
    )
    return image_part, text_part


def first_body(
    scalars, a, b, c, d, text, ahead, behind, third, target,
    image_sum, mine, back_1, back_m1, back_3,
):
    quarter = text.shape[0]
    group = jnp.concatenate([unit_rows(s[...])[0].astype(LOW) for s in (a, b, c, d)])
    units = [unit_rows(s[...])[0] for s in (text, ahead, behind, third)]
    low = jnp.concatenate([u.astype(LOW) for u in units])
    image_part, text_part = meet(group, low, scalars, target[...], (0, 1, -1, 3))
    image_sum[...] = image_part
    parts = [tangent(u, text_part[i * quarter : (i + 1) * quarter]) for i, u in enumerate(units)]
    mine[...] = parts[0]
    back_1[...] = parts[1].astype(LOW)
    back_m1[...] = parts[2].astype(LOW)
    back_3[...] = parts[3].astype(LOW)


def second_body(
    scalars, a, b, c, d, ahead, behind, target, so_far, send, kept, back_2, back_m2
):
    quarter = a.shape[0]
    units = [unit_rows(s[...])[0] for s in (a, b, c, d)]
    group = jnp.concatenate([u.astype(LOW) for u in units])
    text_units = [unit_rows(s[...])[0] for s in (ahead, behind)]
    low = jnp.concatenate([u.astype(LOW) for u in text_units])
    image_part, text_part = meet(group, low, scalars, target[...], (2, -2))
    back_2[...] = tangent(text_units[0], text_part[:quarter]).astype(LOW)
    back_m2[...] = tangent(text_units[1], text_part[quarter:]).astype(LOW)
    total = so_far[...] + image_part
    parts = [tangent(u, total[i * quarter : (i + 1) * quarter]) for i, u in enumerate(units)]
    send[0] = parts[1].astype(LOW)
    send[1] = parts[3].astype(LOW)
    kept[0] = parts[0]
    kept[1] = parts[2]


def merge_body(kept, near, own, far):
    own[...] = kept[0] + near[0].astype(WIDE)
    far[...] = (kept[1] + near[1].astype(WIDE)).astype(LOW)


def image_body(scalars, raw, own, far, out):
    _, inverse = unit_rows(raw[...])
    out[...] = (scalars[0] * inverse) * (own[...] + far[...].astype(WIDE))


def text_body(scalars, raw, mine, *parts):
    *parts, out = parts
    _, inverse = unit_rows(raw[...])
    total = mine[...]
    for part in parts:
        total = total + part[...].astype(WIDE)
    out[...] = (scalars[0] * inverse) * total


def local(images, texts, positive_offset, logit_log_scale, bias):
    quarter, width = texts.shape
    shard, two, four = (quarter, width), (2 * quarter, width), (MEMBERS * quarter, width)
    count = lax.axis_size("dp")
    scalars = jnp.concatenate([jnp.exp(logit_log_scale), bias])
    target = (positive_offset - 2).reshape(1, quarter)

    images_far = from_member(images, 2)
    text = {0: texts}
    text[3] = from_group(texts, 3)
    text[-1] = from_group(texts, -1)
    text[1] = from_group(texts, 1)
    images_near = from_member(images, 1)
    images_far_near = from_member(images_far, 1)
    column = lax.axis_index("dp") % 4
    line = [(i // 4 * 4 + (i - 1) % 4, i) for i in range(count)]
    text[2] = lax.ppermute(jnp.where(column == 3, text[-1], text[3]), "dp", line)
    text[-2] = from_group(text[-1], -1)
    group = (images, images_near, images_far, images_far_near)

    image_sum, mine, back_1, back_m1, back_3 = kernel_call(
        first_body,
        [(four, WIDE), (shard, WIDE), (shard, LOW), (shard, LOW), (shard, LOW)],
        scalars, *group, text[0], text[1], text[-1], text[3], target,
    )
    home_3 = from_group(back_3, -3)
    home_1 = from_group(back_1, -1)
    home_m1 = from_group(back_m1, 1)
    send, kept, back_2, back_m2 = kernel_call(
        second_body,
        [((2, *shard), LOW), ((2, *shard), WIDE), (shard, LOW), (shard, LOW)],
        scalars, *group, text[2], text[-2], target, image_sum,
    )
    near = from_member(send, 1)
    home_2 = from_group(back_2, -2)
    home_m2 = from_group(back_m2, 2)
    own, far = kernel_call(merge_body, [(shard, WIDE), (shard, LOW)], kept, near)
    far = from_member(far, 2)
    (text_gradient,) = kernel_call(
        text_body, [(shard, WIDE)], scalars, texts, mine, home_1, home_m1, home_3, home_2, home_m2
    )
    (image_gradient,) = kernel_call(image_body, [(shard, WIDE)], scalars, images, own, far)
    return image_gradient, text_gradient


def solution(mesh):
    return jax.shard_map(
        local,
        mesh=mesh,
        in_specs=(P(("dp", "rows"), None), P(("dp", "rows"), None), P(("dp", "rows")), P(), P()),
        out_specs=(P(("dp", "rows"), None), P(("dp", "rows"), None)),
        check_vma=False,
    )
```

```python
import jax
import jax.numpy as jnp
from jax import lax
from jax.experimental import pallas as pl
from jax.experimental.pallas import tpu as pltpu
from jax.sharding import PartitionSpec as P

MEMBERS = 4
VMEM = pl.BlockSpec(memory_space=pltpu.VMEM)
SMEM = pl.BlockSpec(memory_space=pltpu.SMEM)
LIMIT = 32 << 20
LOW, WIDE = jnp.bfloat16, jnp.float32


def from_member(block, flip):
    return lax.ppermute(block, "rows", [(i ^ flip, i) for i in range(MEMBERS)])


def from_group(block, distance):
    count = lax.axis_size("dp")
    return lax.ppermute(block, "dp", [((i + distance) % count, i) for i in range(count)])


def kernel_call(body, outs, *args):
    return pl.pallas_call(
        body,
        out_shape=[jax.ShapeDtypeStruct(s, d) for s, d in outs],
        in_specs=[SMEM if a.ndim == 1 else VMEM for a in args],
        out_specs=[VMEM] * len(outs),
        compiler_params=pltpu.CompilerParams(vmem_limit_bytes=LIMIT),
        cost_estimate=pl.CostEstimate(flops=0, bytes_accessed=0, transcendentals=0),
    )(*args)


def unit_rows(raw):
    wide = raw.astype(WIDE)
    inverse = lax.rsqrt(jnp.sum(wide * wide, axis=1, keepdims=True) + 1e-06)
    return wide * inverse, inverse


def tangent(unit, direction):
    return direction - unit * jnp.sum(unit * direction, axis=1, keepdims=True)


def sigmoid(values):
    return 1.0 / (1.0 + jnp.exp(-values))


def meet(group, text, scalars, target, offsets):
    quarter = target.shape[1]
    scores = lax.dot_general(
        group, text, (((1,), (1,)), ((), ())), preferred_element_type=WIDE
    )
    logits = scalars[0] * scores + scalars[1]
    row = lax.broadcasted_iota(jnp.int32, (quarter, quarter), 0)
    diagonal = row == lax.broadcasted_iota(jnp.int32, (quarter, quarter), 1)
    own = []
    for i, offset in enumerate(offsets):
        block = logits[:quarter, i * quarter : (i + 1) * quarter]
        sign = jnp.where(jnp.logical_and(diagonal, target == offset + 2), -1.0, 1.0)
        own.append(sign * sigmoid(sign * block))
    own = jnp.concatenate(own, axis=1).astype(LOW)
    weights = jnp.concatenate([own, sigmoid(logits[quarter:]).astype(LOW)])
    image_part = jnp.dot(weights, text, preferred_element_type=WIDE)
    text_part = lax.dot_general(
        weights, group, (((0,), (0,)), ((), ())), preferred_element_type=WIDE
    )
    return image_part, text_part


def first_body(
    scalars, a, b, c, d, text, ahead, behind, third, target,
    image_sum, mine, back_1, back_m1, back_3,
):
    quarter = text.shape[0]
    group = jnp.concatenate([unit_rows(s[...])[0].astype(LOW) for s in (a, b, c, d)])
    units = [unit_rows(s[...])[0] for s in (text, ahead, behind, third)]
    low = jnp.concatenate([u.astype(LOW) for u in units])
    image_part, text_part = meet(group, low, scalars, target[...], (0, 1, -1, 3))
    image_sum[...] = image_part
    parts = [tangent(u, text_part[i * quarter : (i + 1) * quarter]) for i, u in enumerate(units)]
    mine[...] = parts[0]
    back_1[...] = parts[1].astype(LOW)
    back_m1[...] = parts[2].astype(LOW)
    back_3[...] = parts[3].astype(LOW)


def second_body(
    scalars, a, b, c, d, ahead, behind, target, so_far, send, kept, back_2, back_m2
):
    quarter = a.shape[0]
    units = [unit_rows(s[...])[0] for s in (a, b, c, d)]
    group = jnp.concatenate([u.astype(LOW) for u in units])
    text_units = [unit_rows(s[...])[0] for s in (ahead, behind)]
    low = jnp.concatenate([u.astype(LOW) for u in text_units])
    image_part, text_part = meet(group, low, scalars, target[...], (2, -2))
    back_2[...] = tangent(text_units[0], text_part[:quarter]).astype(LOW)
    back_m2[...] = tangent(text_units[1], text_part[quarter:]).astype(LOW)
    total = so_far[...] + image_part
    parts = [tangent(u, total[i * quarter : (i + 1) * quarter]) for i, u in enumerate(units)]
    send[0] = parts[1].astype(LOW)
    send[1] = parts[3].astype(LOW)
    kept[0] = parts[0]
    kept[1] = parts[2]


def merge_body(kept, near, own, far):
    own[...] = kept[0] + near[0].astype(WIDE)
    far[...] = (kept[1] + near[1].astype(WIDE)).astype(LOW)


def image_body(scalars, raw, own, far, out):
    _, inverse = unit_rows(raw[...])
    out[...] = (scalars[0] * inverse) * (own[...] + far[...].astype(WIDE))


def text_body(scalars, raw, mine, *parts):
    *parts, out = parts
    _, inverse = unit_rows(raw[...])
    total = mine[...]
    for part in parts:
        total = total + part[...].astype(WIDE)
    out[...] = (scalars[0] * inverse) * total


def local(images, texts, positive_offset, logit_log_scale, bias):
    quarter, width = texts.shape
    shard, two, four = (quarter, width), (2 * quarter, width), (MEMBERS * quarter, width)
    count = lax.axis_size("dp")
    scalars = jnp.concatenate([jnp.exp(logit_log_scale), bias])
    target = positive_offset.reshape(1, quarter)

    images_far = from_member(images, 2)
    text = {0: texts}
    text[3] = from_group(texts, 3)
    text[-1] = from_group(texts, -1)
    text[1] = from_group(texts, 1)
    images_near = from_member(images, 1)
    images_far_near = from_member(images_far, 1)
    column = lax.axis_index("dp") % 4
    line = [(i // 4 * 4 + (i - 1) % 4, i) for i in range(count)]
    text[2] = lax.ppermute(jnp.where(column == 3, text[-1], text[3]), "dp", line)
    text[-2] = from_group(text[-1], -1)
    group = (images, images_near, images_far, images_far_near)

    image_sum, mine, back_1, back_m1, back_3 = kernel_call(
        first_body,
        [(four, WIDE), (shard, WIDE), (shard, LOW), (shard, LOW), (shard, LOW)],
        scalars, *group, text[0], text[1], text[-1], text[3], target,
    )
    home_3 = from_group(back_3, -3)
    home_1 = from_group(back_1, -1)
    home_m1 = from_group(back_m1, 1)
    send, kept, back_2, back_m2 = kernel_call(
        second_body,
        [((2, *shard), LOW), ((2, *shard), WIDE), (shard, LOW), (shard, LOW)],
        scalars, *group, text[2], text[-2], target, image_sum,
    )
    near = from_member(send, 1)
    home_2 = from_group(back_2, -2)
    home_m2 = from_group(back_m2, 2)
    own, far = kernel_call(merge_body, [(shard, WIDE), (shard, LOW)], kept, near)
    far = from_member(far, 2)
    (text_gradient,) = kernel_call(
        text_body, [(shard, WIDE)], scalars, texts, mine, home_1, home_m1, home_3, home_2, home_m2
    )
    (image_gradient,) = kernel_call(image_body, [(shard, WIDE)], scalars, images, own, far)
    return image_gradient, text_gradient


def solution(mesh):
    return jax.shard_map(
        local,
        mesh=mesh,
        in_specs=(P(("dp", "rows"), None), P(("dp", "rows"), None), P(("dp", "rows")), P(), P()),
        out_specs=(P(("dp", "rows"), None), P(("dp", "rows"), None)),
        check_vma=False,
    )
```
